32 devices in a mesh: rep: 2 (over y), dp: 4 (over z), tp: 4 (over x, core).
Axes of the slice: x: 2, y: 2, z: 4, core: 2. Of those that a mesh axis runs over, the one named last changes fastest.
Arguments:
- acts: bfloat16 [8192, 5120], P(('rep', 'dp'), 'tp'), parts along dimension 0, may hold values from -6 to 6
- output_gradient: bfloat16 [8192, 1024], P(('rep', 'dp'), 'tp'), parts along dimension 0, may hold values from -6 to 6
- value_matrix: bfloat16 [5120, 1024], P('tp'), may hold values from -0.078125 to 0.078125
- adapter_down_weight: bfloat16 [4, 64, 5120], P('dp', None, 'tp'), may hold values from -0.078125 to 0.078125
- adapter_up_weight: bfloat16 [4, 64, 1024], P('dp', None, 'tp'), may hold values from -0.75 to 0.75
- token_block_job: int32 [64], P(('rep', 'dp')), parts along dimension 0, may hold values from 0 to 3
- block_live_rows: int32 [64], P(('rep', 'dp')), parts along dimension 0, may hold values from 1 to 128, as said below
- job_owner_slot: int32 [4], replicated, may hold values from 0 to 3, each once
Outputs:
- input_gradient: bfloat16 [8192, 5120], P(('rep', 'dp'), 'tp'), parts along dimension 0
- grad_down: float32 [8, 64, 5120], P(('rep', 'dp'), None, 'tp'), parts along dimension 0
- grad_up: float32 [8, 64, 1024], P(('rep', 'dp'), None, 'tp'), parts along dimension 0
The draws below stay inside these ranges and needn't reach their ends.
There are 2 independent parts, one for each index of `rep`. The reference program is written for one: setup_inputs(seed, part) draws one part's arguments, and reference() takes and returns one part's arrays. A program takes and returns all parts, laid end to end along the dimension named above; an argument that names none is the same for every part. Nothing has to cross between parts.
Inputs may be any that keep to these rules, and one draw needn't show every extreme that they name: `block_live_rows`: some block of every draw is full.
All inputs are finite; a program needn't handle non-finite values.
Results may differ from the reference program's by a relative error of at most 0.017.
Values may be sent and summed in bfloat16 or wider, within the bound.
A program may use at most 64 MiB of HBM per device.

```python
import math
import jax
import jax.numpy as jnp
import numpy as np
from jax import lax

MODEL_WIDTH = 5120
ADAPTER_RANK = 64
BLOCK_ROW_COUNT = 128
TOKEN_BLOCKS = 8
VALUE_FEATURES = 1024
ADAPTER_JOBS = 4
BLOCKS = 32
ROWS = 4096
N_DP = 4


def draw_block_live_rows(key, part):
    key = jax.random.fold_in(key, 11)
    first_key, second_key = jax.random.split(key)
    full_flag = jax.random.randint(first_key, (BLOCKS,), 0, 2)
    partial_rows = jax.random.randint(second_key, (BLOCKS,), 1, BLOCK_ROW_COUNT + 1)
    partial_rows = partial_rows.at[0].set(BLOCK_ROW_COUNT)
    return jnp.where(full_flag == 1, BLOCK_ROW_COUNT, partial_rows).astype(jnp.int32)


def set_ends(array, stream_key, least, top_value):
    spot = [jax.random.randint(jax.random.fold_in(stream_key, axis), (), 0, length) for axis, length in enumerate(array.shape)]
    widest = array.shape.index(max(array.shape))
    next_to = spot[:widest] + [(spot[widest] + 1) % array.shape[widest]] + spot[widest + 1:]
    return array.at[tuple(spot)].set(least).at[tuple(next_to)].set(top_value)


def block_levels(own_key, dims, cuts, low, largest):
    level, own = 1.0, jax.random.fold_in(own_key, 6)
    for dim, blocks in cuts:
        heights = jnp.exp(jax.random.uniform(jax.random.fold_in(own, dim), (blocks,), jnp.float32, low / len(cuts), largest / len(cuts)))
        level = level * jnp.repeat(heights, dims[dim] // blocks).reshape([-1 if axis == dim else 1 for axis in range(len(dims))])
    return level


def rank_table(count, slope):
    loads = [(1 << 20) // math.isqrt(grade ** slope) + 1 for grade in range(1, count + 1)]
    spread = 1 + sum(loads) // (1 << 30)
    return np.cumsum(np.array([max(1, weight // spread) for weight in loads]))


def ranked_ids(key, extent, number_of, lean):
    table = rank_table(number_of, lean)
    pick = jax.random.randint(jax.random.fold_in(key, 1), extent, 0, int(table[number_of - 1]))
    grade = jnp.searchsorted(jnp.asarray(table, jnp.int32), pick, side="right")
    return jax.random.permutation(jax.random.fold_in(key, 2), number_of)[grade].astype(jnp.int32)


def bell_draw(key, shape, scale, most, pieces=(), held_as=jnp.bfloat16):
    drawn = scale * jax.random.normal(key, shape, jnp.float32)
    if pieces:
        drawn = drawn * block_levels(key, shape, pieces, -0.22, 0.18)
    return jnp.clip(drawn, -most, most).astype(held_as)


def setup_inputs(seed: int = 0, part: int = 0) -> dict:
    seeds = jax.random.split(jax.random.key(seed), 9)
    part_splits = jax.random.split(jax.random.fold_in(seeds[8], part), 9)
    return {
        "acts": bell_draw(part_splits[0], (ROWS, MODEL_WIDTH), 1.0, 6.0, ((0, 4), (1, 4))),
        "output_gradient": bell_draw(part_splits[1], (ROWS, VALUE_FEATURES), 1.0, 6.0, ((0, 4), (1, 4))),
        "value_matrix": bell_draw(seeds[2], (MODEL_WIDTH, VALUE_FEATURES), MODEL_WIDTH ** -0.5, 0.078125, ((0, 4),)),
        "adapter_down_weight": bell_draw(seeds[3], (ADAPTER_JOBS, ADAPTER_RANK, MODEL_WIDTH), MODEL_WIDTH ** -0.5, 0.078125, ((0, 4), (2, 4))),
        "adapter_up_weight": bell_draw(seeds[4], (ADAPTER_JOBS, ADAPTER_RANK, VALUE_FEATURES), ADAPTER_RANK ** -0.5, 0.75, ((0, 4), (2, 4))),
        "token_block_job": set_ends(ranked_ids(part_splits[5], (BLOCKS,), ADAPTER_JOBS, 2), jax.random.fold_in(part_splits[5], 3), 0, ADAPTER_JOBS - 1).astype(jnp.int32),
        "block_live_rows": draw_block_live_rows(jax.random.fold_in(jax.random.fold_in(seeds[8], part), 71), part),
        "job_owner_slot": jax.random.permutation(seeds[7], ADAPTER_JOBS).astype(jnp.int32),
    }


adapter_scale = 2.0


def reference(acts, output_gradient, value_matrix, adapter_down_weight, adapter_up_weight, token_block_job, block_live_rows, job_owner_slot):
    block_slot = job_owner_slot[token_block_job].astype(jnp.int32)
    live_rows = jnp.arange(BLOCK_ROW_COUNT, dtype=jnp.int32)[None, :] < block_live_rows[:, None]
    cotangent = jnp.where(live_rows.reshape(ROWS, 1), output_gradient, jnp.zeros((), jnp.bfloat16))
    act_groups = acts.reshape(N_DP, TOKEN_BLOCKS, BLOCK_ROW_COUNT, MODEL_WIDTH)
    cot_groups = cotangent.reshape(N_DP, TOKEN_BLOCKS, BLOCK_ROW_COUNT, VALUE_FEATURES)
    slot_groups = block_slot.reshape(N_DP, TOKEN_BLOCKS)
    weight_full = value_matrix.astype(jnp.float32)
    upper_bound = lax.Precision.HIGHEST

    def one_group(running, item):
        act_blocks, cot_blocks, group_position = item
        chosen_down = adapter_down_weight[group_position].astype(jnp.float32)
        chosen_up = adapter_up_weight[group_position].astype(jnp.float32)
        input_wide = act_blocks.astype(jnp.float32)
        output_gradient_wide = cot_blocks.astype(jnp.float32)
        rank_projection = jnp.einsum('bid,brd->bir', input_wide, chosen_down, precision=upper_bound).astype(jnp.bfloat16)
        backward_projection = jnp.einsum('bik,brk->bir', output_gradient_wide, chosen_up, precision=upper_bound).astype(jnp.bfloat16)
        frozen_gradient = jnp.dot(output_gradient_wide.reshape(TOKEN_BLOCKS * BLOCK_ROW_COUNT, VALUE_FEATURES), weight_full.T, precision=upper_bound)
        adapter_gradient = jnp.einsum('bir,brd->bid', backward_projection.astype(jnp.float32), chosen_down, precision=upper_bound)
        gradient_rows = (frozen_gradient + adapter_scale * adapter_gradient.reshape(TOKEN_BLOCKS * BLOCK_ROW_COUNT, MODEL_WIDTH)).astype(jnp.bfloat16)
        down_matrix_block = adapter_scale * jnp.einsum('lwe,lwf->lef', backward_projection.astype(jnp.float32), input_wide, precision=upper_bound)
        up_matrix_block = adapter_scale * jnp.einsum('txh,txn->thn', rank_projection.astype(jnp.float32), output_gradient_wide, precision=upper_bound)
        one_hot = (group_position[None, :] == jnp.arange(ADAPTER_JOBS, dtype=jnp.int32)[:, None]).astype(jnp.float32)
        down_part = jnp.einsum('jb,brd->jrd', one_hot, down_matrix_block, precision=upper_bound).astype(jnp.bfloat16)
        up_part = jnp.einsum('jb,brk->jrk', one_hot, up_matrix_block, precision=upper_bound).astype(jnp.bfloat16)
        return (running[0] + down_part.astype(jnp.float32), running[1] + up_part.astype(jnp.float32)), gradient_rows

    zero_down = jnp.zeros((ADAPTER_JOBS, ADAPTER_RANK, MODEL_WIDTH), jnp.float32)
    zero_up = jnp.zeros((ADAPTER_JOBS, ADAPTER_RANK, VALUE_FEATURES), jnp.float32)
    (grad_down, grad_up), grad_groups = lax.scan(one_group, (zero_down, zero_up), (act_groups, cot_groups, slot_groups))
    return grad_groups.reshape(ROWS, MODEL_WIDTH), grad_down, grad_up
```

```python
import functools

import jax
import jax.numpy as jnp
from jax import lax
from jax.experimental import pallas as pl
from jax.experimental.pallas import tpu as pltpu
from jax.sharding import PartitionSpec as P

adapter_scale = 2.0
cot_chunks = 4
early_chunks = 2
f32 = jnp.float32
bf16 = jnp.bfloat16
MESH = pl.DeviceIdType.MESH
nt = (((1,), (1,)), ((), ()))
nn = (((1,), (0,)), ((), ()))
tn = (((0,), (0,)), ((), ()))


def dot(a, b, dims):
    return lax.dot_general(a, b, dims, preferred_element_type=f32)


def send(src, dst, send_sem, recv_sem, **device):
    return pltpu.make_async_remote_copy(
        src_ref=src,
        dst_ref=dst,
        send_sem=send_sem,
        recv_sem=recv_sem,
        device_id=device,
        device_id_type=MESH,
    )


def kernel(
    reps, owners, parts_tp,
    acts, grad, matrix, down, up, job, live, owner_slot,
    out, grad_down, grad_up,
    act_v, mat_v, cot_v, down_v, up_v,
    back_p, low_p, back_d, back_m, low_m,
    pdown, pup, rdown, rup,
    load_sem, up_s, up_r, dn_s, dn_r, yf_s, yf_r,
    ch_s, ch_r, cl_s, cl_r, cf_s, cf_r,
    bk_s, bk_r, lw_s, lw_r, pd_s, pd_r, pu_s, pu_r,
):
    r = lax.axis_index("rep")
    d = lax.axis_index("dp")
    t = lax.axis_index("tp")
    rows, width = act_v.shape
    rank = down_v.shape[1]
    blocks = job.shape[0]
    block = rows // blocks
    half = blocks // 2
    highs = parts_tp // 2
    hi, lo = t // 2, t % 2
    other = hi * 2 + 1 - lo
    share = rank // reps
    chunk = rows // cot_chunks
    stages = parts_tp.bit_length() - 1

    loads = [
        pltpu.make_async_copy(src, dst, load_sem.at[i])
        for i, (src, dst) in enumerate(
            [
                (up.at[0], up_v.at[d]),
                (grad, cot_v.at[t]),
                (down.at[0], down_v.at[d]),
                (acts, act_v),
                (matrix, mat_v),
            ]
        )
    ]
    for load in loads:
        load.start()

    barrier = pltpu.get_barrier_semaphore()
    peers = [{"dp": (d + j) % owners} for j in range(1, owners)]
    peers += [{"tp": ((hi + i) % highs) * 2 + lo} for i in range(1, highs)]
    peers += [{"tp": other}]
    peers += [{"rep": (r + i) % reps} for i in range(1, reps)]
    for peer in peers:
        pl.semaphore_signal(barrier, inc=1, device_id=peer, device_id_type=MESH)
    pl.semaphore_wait(barrier, len(peers))

    up_out = [
        send(up.at[0], up_v.at[d], up_s.at[j], up_r.at[j], dp=(d + j) % owners)
        for j in range(1, owners)
    ]
    for copy in up_out:
        copy.start()

    def cot_rows(c):
        return pl.ds(c * chunk, chunk)

    cot_out = [
        [
            send(
                grad.at[cot_rows(c)], cot_v.at[t, cot_rows(c)], ch_s.at[i, c], ch_r.at[i, c],
                tp=((hi + i) % highs) * 2 + lo,
            )
            for i in range(1, highs)
        ]
        for c in range(cot_chunks)
    ]
    cot_near = send(grad, cot_v.at[t], cl_s, cl_r, tp=other)
    for c in range(early_chunks):
        for copy in cot_out[c]:
            copy.start()
    cot_near.start()

    mine = pl.ds(r * share, share)
    dn_out = [
        send(
            down.at[0, mine], down_v.at[d, mine], dn_s.at[j], dn_r.at[j], dp=(d + j) % owners
        )
        for j in range(1, owners)
    ]
    for copy in dn_out:
        copy.start()

    slots = [owner_slot[job[b]] for b in range(blocks)]
    lives = [live[b] for b in range(blocks)]

    def stage_copy(buf, s, ss, rs):
        step = 1 << s
        partner = t + step * (1 - 2 * ((t // step) % 2))
        return send(buf.at[2 * s], buf.at[2 * s + 1], ss.at[s], rs.at[s], tp=partner)

    def pack(buf, source, weights, columns):
        for b in range(half):
            pair = []
            for q in (b, b + half):
                weight = weights[slots[q]]
                pair.append(dot(source[pl.ds(q * block, block), :], weight, nt))
            buf[0, pl.ds(b * block, block), :] = jnp.concatenate(pair, 1).astype(bf16)

    def fold(buf, s):
        total = buf[2 * s].astype(f32) + buf[2 * s + 1].astype(f32)
        buf[2 * s + 2] = total.astype(bf16)

    def spread(buf, wide, doubled):
        packed = buf.at[2 * stages]
        for b in range(half):
            pair = packed[pl.ds(b * block, block), :].astype(f32)
            for q, v in ((b, pair[:, :rank]), (b + half, pair[:, rank:])):
                two = jnp.concatenate([v, v], 1)
                rows_q = pl.ds(q * block, block)
                if doubled is not None:
                    doubled[rows_q, :] = two.astype(bf16)
                shape = (block, 2 * rank)
                alive = lax.broadcasted_iota(jnp.int32, shape, 0) < lives[q]
                lane = lax.broadcasted_iota(jnp.int32, shape, 1)
                odd = jnp.where(lane >= rank, 1, 0)
                for k in range(0, owners, 2):
                    keep = jnp.logical_and(alive, odd + k == slots[q])
                    wide[rows_q, pl.ds(k * rank, 2 * rank)] = jnp.where(keep, two, 0.0).astype(bf16)

    loads[0].wait()
    loads[1].wait()
    for j in range(1, owners):
        src = (d + owners - j) % owners
        send(up.at[0], up_v.at[src], up_s.at[j], up_r.at[j], dp=src).wait_recv()
    pack(back_p, cot_v.at[t], up_v, None)
    stage_copy(back_p, 0, bk_s, bk_r).start()
    for s in range(stages):
        stage_copy(back_p, s, bk_s, bk_r).wait()
        fold(back_p, s)
        if s + 1 < stages:
            stage_copy(back_p, s + 1, bk_s, bk_r).start()
        if s == 0:
            for c in range(early_chunks, cot_chunks):
                for copy in cot_out[c]:
                    copy.start()
    spread(back_p, back_m, back_d)

    group = min(owners, 4)
    loads[3].wait()
    for g in range(0, owners, group):
        lhs = back_m[:, pl.ds(g * rank, group * rank)]
        block_part = adapter_scale * dot(lhs, act_v[...], tn)
        pdown[pl.ds(g, group)] = block_part.astype(bf16).reshape(group, rank, width)
    pd_out = [
        send(
            pdown.at[(d + j) % owners], rdown.at[d], pd_s.at[j], pd_r.at[j], dp=(d + j) % owners
        )
        for j in range(1, owners)
    ]
    for copy in pd_out:
        copy.start()

    loads[2].wait()
    forwards = []
    for j in range(1, owners):
        src = (d + owners - j) % owners
        send(down.at[0, mine], down_v.at[src, mine], dn_s.at[j], dn_r.at[j], dp=src).wait_recv()
        for i in range(1, reps):
            copy = send(
                down_v.at[src, mine], down_v.at[src, mine], yf_s.at[i, j], yf_r.at[i, j],
                rep=(r + i) % reps,
            )
            copy.start()
            forwards.append(copy)

    for c in range(cot_chunks):
        for i in range(1, highs):
            src = ((hi + highs - i) % highs) * 2 + lo
            there = cot_v.at[src, cot_rows(c)]
            send(grad.at[cot_rows(c)], there, ch_s.at[i, c], ch_r.at[i, c], tp=src).wait_recv()
            copy = send(there, there, cf_s.at[i, c], cf_r.at[i, c], tp=other)
            copy.start()
            forwards.append(copy)

    for j in range(1, owners):
        src = (d + owners - j) % owners
        for i in range(1, reps):
            giver = (r + reps - i) % reps
            theirs = down_v.at[src, pl.ds(giver * share, share)]
            send(theirs, theirs, yf_s.at[i, j], yf_r.at[i, j], rep=giver).wait_recv()

    pack(low_p, act_v, down_v, None)
    stage_copy(low_p, 0, lw_s, lw_r).start()

    loads[4].wait()
    cot_near_in = send(grad, cot_v.at[other], cl_s, cl_r, tp=other)
    cot_near_in.wait_recv()
    for c in range(cot_chunks):
        for i in range(1, highs):
            src = ((hi + highs - i) % highs) * 2 + 1 - lo
            there = cot_v.at[src, cot_rows(c)]
            send(there, there, cf_s.at[i, c], cf_r.at[i, c], tp=other).wait_recv()

    def frozen(first, last):
        @pl.loop(first, last)
        def _(b):
            rows_b = pl.ds(pl.multiple_of(b * block, block), block)
            features = jnp.concatenate([cot_v[p, rows_b, :] for p in range(parts_tp)], 1)
            slot = owner_slot[job[b]]
            total = dot(features, mat_v[...], nt)
            total += adapter_scale * dot(back_d[rows_b, :][:, :rank], down_v[slot], nn)
            alive = lax.broadcasted_iota(jnp.int32, (block, width), 0) < live[b]
            out[rows_b, :] = jnp.where(alive, total, 0.0).astype(bf16)

    bounds = [blocks * s // (stages + 1) for s in range(stages + 2)]
    for s in range(stages):
        frozen(bounds[s], bounds[s + 1])
        stage_copy(low_p, s, lw_s, lw_r).wait()
        fold(low_p, s)
        if s + 1 < stages:
            stage_copy(low_p, s + 1, lw_s, lw_r).start()
    spread(low_p, low_m, None)

    for g in range(0, owners, group):
        lhs = low_m[:, pl.ds(g * rank, group * rank)]
        block_part = adapter_scale * dot(lhs, cot_v[t], tn)
        pup[pl.ds(g, group)] = block_part.astype(bf16).reshape(group, rank, up_v.shape[2])
    pu_out = [
        send(pup.at[(d + j) % owners], rup.at[d], pu_s.at[j], pu_r.at[j], dp=(d + j) % owners)
        for j in range(1, owners)
    ]
    for copy in pu_out:
        copy.start()
    frozen(bounds[stages], bounds[stages + 1])

    for mine_part, got, ss, rs, result in (
        (pdown, rdown, pd_s, pd_r, grad_down),
        (pup, rup, pu_s, pu_r, grad_up),
    ):
        total = mine_part[d].astype(f32)
        for j in range(1, owners):
            src = (d + owners - j) % owners
            send(mine_part.at[src], got.at[src], ss.at[j], rs.at[j], dp=src).wait_recv()
            total += got[src].astype(f32)
        result[0] = total

    for copy in up_out + dn_out + pd_out + pu_out + forwards + [cot_near]:
        copy.wait_send()
    for copies in cot_out:
        for copy in copies:
            copy.wait_send()


def solution(mesh):
    reps, owners, parts_tp = mesh.shape["rep"], mesh.shape["dp"], mesh.shape["tp"]

    def body(acts, grad, matrix, down, up, job, live, owner_slot):
        rows, width = acts.shape
        features = grad.shape[1]
        rank = down.shape[1]
        stages = parts_tp.bit_length() - 1
        highs = parts_tp // 2
        vmem = pltpu.VMEM
        dma = pltpu.SemaphoreType.DMA
        any_space = pl.BlockSpec(memory_space=pl.ANY)
        smem = pl.BlockSpec(memory_space=pltpu.SMEM)
        in_vmem = pl.BlockSpec(memory_space=pltpu.VMEM)
        packed = vmem((2 * stages + 1, rows // 2, 2 * rank), bf16)
        return pl.pallas_call(
            functools.partial(kernel, reps, owners, parts_tp),
            out_shape=(
                jax.ShapeDtypeStruct((rows, width), bf16),
                jax.ShapeDtypeStruct((1, rank, width), f32),
                jax.ShapeDtypeStruct((1, rank, features), f32),
            ),
            in_specs=[any_space] * 5 + [smem] * 3,
            out_specs=(in_vmem,) * 3,
            scratch_shapes=[
                vmem((rows, width), bf16),
                vmem(matrix.shape, bf16),
                vmem((parts_tp, rows, features), bf16),
                vmem((owners, rank, width), bf16),
                vmem((owners, rank, features), bf16),
                packed,
                packed,
                vmem((rows, 2 * rank), bf16),
                vmem((rows, owners * rank), bf16),
                vmem((rows, owners * rank), bf16),
                vmem((owners, rank, width), bf16),
                vmem((owners, rank, features), bf16),
                vmem((owners, rank, width), bf16),
                vmem((owners, rank, features), bf16),
                dma((5,)),
                dma((owners,)), dma((owners,)),
                dma((owners,)), dma((owners,)),
                dma((reps, owners)), dma((reps, owners)),
                dma((highs, cot_chunks)), dma((highs, cot_chunks)),
                dma, dma,
                dma((highs, cot_chunks)), dma((highs, cot_chunks)),
                dma((stages,)), dma((stages,)),
                dma((stages,)), dma((stages,)),
                dma((owners,)), dma((owners,)),
                dma((owners,)), dma((owners,)),
            ],
            compiler_params=pltpu.CompilerParams(
                collective_id=0, has_side_effects=True, vmem_limit_bytes=48 * 1024 * 1024
            ),
            name="lora_value_backward",
        )(acts, grad, matrix, down, up, job, live, owner_slot)

    placed = (
        P(("rep", "dp"), "tp"),
        P(("rep", "dp"), "tp"),
        P("tp", None),
        P("dp", None, "tp"),
        P("dp", None, "tp"),
        P(("rep", "dp")),
        P(("rep", "dp")),
        P(),
    )
    return jax.shard_map(
        body,
        mesh=mesh,
        in_specs=placed,
        out_specs=(
            P(("rep", "dp"), "tp"),
            P(("rep", "dp"), None, "tp"),
            P(("rep", "dp"), None, "tp"),
        ),
        check_vma=False,
    )
```

```python
import functools

import jax
import jax.numpy as jnp
from jax import lax
from jax.experimental import pallas as pl
from jax.experimental.pallas import tpu as pltpu
from jax.sharding import PartitionSpec as P

adapter_scale = 2.0
cot_chunks = 4
early_chunks = 2
write_pieces = 8
vmem_bytes = 56 * 1024 * 1024
f32 = jnp.float32
bf16 = jnp.bfloat16
MESH = pl.DeviceIdType.MESH
nt = (((1,), (1,)), ((), ()))
nn = (((1,), (0,)), ((), ()))
tn = (((0,), (0,)), ((), ()))


def dot(a, b, dims):
    return lax.dot_general(a, b, dims, preferred_element_type=f32)


def send(src, dst, send_sem, recv_sem, **device):
    return pltpu.make_async_remote_copy(
        src_ref=src,
        dst_ref=dst,
        send_sem=send_sem,
        recv_sem=recv_sem,
        device_id=device,
        device_id_type=MESH,
    )


def kernel(
    reps, owners, parts_tp,
    acts, grad, matrix, down, up, job_h, live_h, owner_slot_h,
    out, grad_down, grad_up,
    job, live, owner_slot, out_v, out_s, act_v, mat_v, cot_v, down_v, up_v,
    back_p, low_p, back_d, back_m, low_m,
    pdown, pup, rdown, rup,
    load_sem, up_s, up_r, dn_s, dn_r, yf_s, yf_r,
    ch_s, ch_r, cl_s, cl_r, cf_s, cf_r,
    bk_s, bk_r, lw_s, lw_r, pd_s, pd_r, pu_s, pu_r,
):
    r = lax.axis_index("rep")
    d = lax.axis_index("dp")
    t = lax.axis_index("tp")
    rows, width = act_v.shape
    rank = down_v.shape[1]
    blocks = job.shape[0]
    block = rows // blocks
    half = blocks // 2
    highs = parts_tp // 2
    hi, lo = t // 2, t % 2
    other = hi * 2 + 1 - lo
    share = rank // reps
    chunk = rows // cot_chunks
    stages = parts_tp.bit_length() - 1

    loads = [
        pltpu.make_async_copy(src, dst, load_sem.at[i])
        for i, (src, dst) in enumerate(
            [
                (job_h, job),
                (live_h, live),
                (owner_slot_h, owner_slot),
                (up.at[0], up_v.at[d]),
                (grad, cot_v.at[t]),
                (down.at[0], down_v.at[d]),
                (acts, act_v),
                (matrix, mat_v),
            ]
        )
    ]
    for load in loads:
        load.start()

    barrier = pltpu.get_barrier_semaphore()
    peers = [{"dp": (d + j) % owners} for j in range(1, owners)]
    peers += [{"tp": ((hi + i) % highs) * 2 + lo} for i in range(1, highs)]
    peers += [{"tp": other}]
    peers += [{"rep": (r + i) % reps} for i in range(1, reps)]
    for peer in peers:
        pl.semaphore_signal(barrier, inc=1, device_id=peer, device_id_type=MESH)
    pl.semaphore_wait(barrier, len(peers))

    up_out = [
        send(up.at[0], up_v.at[d], up_s.at[j], up_r.at[j], dp=(d + j) % owners)
        for j in range(1, owners)
    ]
    for copy in up_out:
        copy.start()

    def cot_rows(c):
        return pl.ds(c * chunk, chunk)

    cot_out = [
        [
            send(
                grad.at[cot_rows(c)], cot_v.at[t, cot_rows(c)], ch_s.at[i, c], ch_r.at[i, c],
                tp=((hi + i) % highs) * 2 + lo,
            )
            for i in range(1, highs)
        ]
        for c in range(cot_chunks)
    ]
    cot_near = send(grad, cot_v.at[t], cl_s, cl_r, tp=other)
    for c in range(early_chunks):
        for copy in cot_out[c]:
            copy.start()
    cot_near.start()

    mine = pl.ds(r * share, share)
    dn_out = [
        send(
            down.at[0, mine], down_v.at[d, mine], dn_s.at[j], dn_r.at[j], dp=(d + j) % owners
        )
        for j in range(1, owners)
    ]
    for copy in dn_out:
        copy.start()

    for load in loads[:5]:
        load.wait()
    slots = [owner_slot[job[b]] for b in range(blocks)]
    lives = [live[b] for b in range(blocks)]

    def stage_copy(buf, s, ss, rs):
        step = 1 << s
        partner = t + step * (1 - 2 * ((t // step) % 2))
        return send(buf.at[2 * s], buf.at[2 * s + 1], ss.at[s], rs.at[s], tp=partner)

    def pack(buf, source, weights, columns):
        for b in range(half):
            pair = []
            for q in (b, b + half):
                weight = weights[slots[q]]
                pair.append(dot(source[pl.ds(q * block, block), :], weight, nt))
            buf[0, pl.ds(b * block, block), :] = jnp.concatenate(pair, 1).astype(bf16)

    def fold(buf, s):
        total = buf[2 * s].astype(f32) + buf[2 * s + 1].astype(f32)
        buf[2 * s + 2] = total.astype(bf16)

    def spread(buf, wide, doubled):
        packed = buf.at[2 * stages]
        for b in range(half):
            pair = packed[pl.ds(b * block, block), :].astype(f32)
            for q, v in ((b, pair[:, :rank]), (b + half, pair[:, rank:])):
                two = jnp.concatenate([v, v], 1)
                rows_q = pl.ds(q * block, block)
                if doubled is not None:
                    doubled[rows_q, :] = two.astype(bf16)
                shape = (block, 2 * rank)
                alive = lax.broadcasted_iota(jnp.int32, shape, 0) < lives[q]
                lane = lax.broadcasted_iota(jnp.int32, shape, 1)
                odd = jnp.where(lane >= rank, 1, 0)
                for k in range(0, owners, 2):
                    keep = jnp.logical_and(alive, odd + k == slots[q])
                    wide[rows_q, pl.ds(k * rank, 2 * rank)] = jnp.where(keep, two, 0.0).astype(bf16)

    for j in range(1, owners):
        src = (d + owners - j) % owners
        send(up.at[0], up_v.at[src], up_s.at[j], up_r.at[j], dp=src).wait_recv()
    pack(back_p, cot_v.at[t], up_v, None)
    stage_copy(back_p, 0, bk_s, bk_r).start()
    for s in range(stages):
        stage_copy(back_p, s, bk_s, bk_r).wait()
        fold(back_p, s)
        if s + 1 < stages:
            stage_copy(back_p, s + 1, bk_s, bk_r).start()
        if s == 0:
            for c in range(early_chunks, cot_chunks):
                for copy in cot_out[c]:
                    copy.start()
    spread(back_p, back_m, back_d)

    group = min(owners, 4)
    loads[6].wait()
    for g in range(0, owners, group):
        lhs = back_m[:, pl.ds(g * rank, group * rank)]
        block_part = adapter_scale * dot(lhs, act_v[...], tn)
        pdown[pl.ds(g, group)] = block_part.astype(bf16).reshape(group, rank, width)
    pd_out = [
        send(
            pdown.at[(d + j) % owners], rdown.at[d], pd_s.at[j], pd_r.at[j], dp=(d + j) % owners
        )
        for j in range(1, owners)
    ]
    for copy in pd_out:
        copy.start()

    loads[5].wait()
    forwards = []
    for j in range(1, owners):
        src = (d + owners - j) % owners
        send(down.at[0, mine], down_v.at[src, mine], dn_s.at[j], dn_r.at[j], dp=src).wait_recv()
        for i in range(1, reps):
            copy = send(
                down_v.at[src, mine], down_v.at[src, mine], yf_s.at[i, j], yf_r.at[i, j],
                rep=(r + i) % reps,
            )
            copy.start()
            forwards.append(copy)

    for c in range(cot_chunks):
        for i in range(1, highs):
            src = ((hi + highs - i) % highs) * 2 + lo
            there = cot_v.at[src, cot_rows(c)]
            send(grad.at[cot_rows(c)], there, ch_s.at[i, c], ch_r.at[i, c], tp=src).wait_recv()
            copy = send(there, there, cf_s.at[i, c], cf_r.at[i, c], tp=other)
            copy.start()
            forwards.append(copy)

    for j in range(1, owners):
        src = (d + owners - j) % owners
        for i in range(1, reps):
            giver = (r + reps - i) % reps
            theirs = down_v.at[src, pl.ds(giver * share, share)]
            send(theirs, theirs, yf_s.at[i, j], yf_r.at[i, j], rep=giver).wait_recv()

    pack(low_p, act_v, down_v, None)
    stage_copy(low_p, 0, lw_s, lw_r).start()

    loads[7].wait()
    cot_near_in = send(grad, cot_v.at[other], cl_s, cl_r, tp=other)
    cot_near_in.wait_recv()
    for c in range(cot_chunks):
        for i in range(1, highs):
            src = ((hi + highs - i) % highs) * 2 + 1 - lo
            there = cot_v.at[src, cot_rows(c)]
            send(there, there, cf_s.at[i, c], cf_r.at[i, c], tp=other).wait_recv()

    def frozen(first, last):
        @pl.loop(first, last)
        def _(b):
            rows_b = pl.ds(pl.multiple_of(b * block, block), block)
            features = jnp.concatenate([cot_v[p, rows_b, :] for p in range(parts_tp)], 1)
            slot = owner_slot[job[b]]
            total = dot(features, mat_v[...], nt)
            total += adapter_scale * dot(back_d[rows_b, :][:, :rank], down_v[slot], nn)
            alive = lax.broadcasted_iota(jnp.int32, (block, width), 0) < live[b]
            out_v[rows_b, :] = jnp.where(alive, total, 0.0).astype(bf16)
            pltpu.make_async_copy(out_v.at[rows_b], out.at[rows_b], out_s.at[b]).start()

    bounds = [blocks * s // (stages + 1) for s in range(stages + 2)]
    for s in range(stages):
        frozen(bounds[s], bounds[s + 1])
        stage_copy(low_p, s, lw_s, lw_r).wait()
        fold(low_p, s)
        if s + 1 < stages:
            stage_copy(low_p, s + 1, lw_s, lw_r).start()
    spread(low_p, low_m, None)

    for g in range(0, owners, group):
        lhs = low_m[:, pl.ds(g * rank, group * rank)]
        block_part = adapter_scale * dot(lhs, cot_v[t], tn)
        pup[pl.ds(g, group)] = block_part.astype(bf16).reshape(group, rank, up_v.shape[2])
    pu_out = [
        send(pup.at[(d + j) % owners], rup.at[d], pu_s.at[j], pu_r.at[j], dp=(d + j) % owners)
        for j in range(1, owners)
    ]
    for copy in pu_out:
        copy.start()
    frozen(bounds[stages], bounds[stages + 1])

    for mine_part, got, ss, rs, result in (
        (pdown, rdown, pd_s, pd_r, grad_down),
        (pup, rup, pu_s, pu_r, grad_up),
    ):
        total = mine_part[d].astype(f32)
        for j in range(1, owners):
            src = (d + owners - j) % owners
            send(mine_part.at[src], got.at[src], ss.at[j], rs.at[j], dp=src).wait_recv()
            total += got[src].astype(f32)
        result[0] = total

    for b in range(blocks):
        rows_b = pl.ds(b * block, block)
        pltpu.make_async_copy(out_v.at[rows_b], out.at[rows_b], out_s.at[b]).wait()
    for copy in up_out + dn_out + pd_out + pu_out + forwards + [cot_near]:
        copy.wait_send()
    for copies in cot_out:
        for copy in copies:
            copy.wait_send()


def write_out(pieces, out_k, down_k, up_k, out, grad_down, grad_up, sem):
    rows = out_k.shape[0] // pieces
    parts = [pl.ds(i * rows, rows) for i in range(pieces)]
    pairs = [(out_k.at[part], out.at[part]) for part in parts]
    pairs += [(down_k, grad_down), (up_k, grad_up)]
    copies = [
        pltpu.make_async_copy(src, dst, sem.at[i]) for i, (src, dst) in enumerate(pairs)
    ]
    for copy in copies:
        copy.start()
    for copy in copies:
        copy.wait()


def solution(mesh):
    reps, owners, parts_tp = mesh.shape["rep"], mesh.shape["dp"], mesh.shape["tp"]

    def body(acts, grad, matrix, down, up, job, live, owner_slot):
        rows, width = acts.shape
        features = grad.shape[1]
        rank = down.shape[1]
        stages = parts_tp.bit_length() - 1
        highs = parts_tp // 2
        vmem = pltpu.VMEM
        dma = pltpu.SemaphoreType.DMA
        in_hbm = pl.BlockSpec(memory_space=pltpu.HBM)
        in_vmem = pl.BlockSpec(memory_space=pltpu.VMEM)
        packed = vmem((2 * stages + 1, rows // 2, 2 * rank), bf16)
        results = pl.pallas_call(
            functools.partial(kernel, reps, owners, parts_tp),
            out_shape=(
                jax.ShapeDtypeStruct((rows, width), bf16),
                jax.ShapeDtypeStruct((1, rank, width), f32),
                jax.ShapeDtypeStruct((1, rank, features), f32),
            ),
            in_specs=[in_hbm] * 8,
            out_specs=(in_hbm, in_vmem, in_vmem),
            scratch_shapes=[
                pltpu.SMEM(job.shape, jnp.int32),
                pltpu.SMEM(live.shape, jnp.int32),
                pltpu.SMEM(owner_slot.shape, jnp.int32),
                vmem((rows, width), bf16),
                dma(job.shape),
                vmem((rows, width), bf16),
                vmem(matrix.shape, bf16),
                vmem((parts_tp, rows, features), bf16),
                vmem((owners, rank, width), bf16),
                vmem((owners, rank, features), bf16),
                packed,
                packed,
                vmem((rows, 2 * rank), bf16),
                vmem((rows, owners * rank), bf16),
                vmem((rows, owners * rank), bf16),
                vmem((owners, rank, width), bf16),
                vmem((owners, rank, features), bf16),
                vmem((owners, rank, width), bf16),
                vmem((owners, rank, features), bf16),
                dma((8,)),
                dma((owners,)), dma((owners,)),
                dma((owners,)), dma((owners,)),
                dma((reps, owners)), dma((reps, owners)),
                dma((highs, cot_chunks)), dma((highs, cot_chunks)),
                dma, dma,
                dma((highs, cot_chunks)), dma((highs, cot_chunks)),
                dma((stages,)), dma((stages,)),
                dma((stages,)), dma((stages,)),
                dma((owners,)), dma((owners,)),
                dma((owners,)), dma((owners,)),
            ],
            compiler_params=pltpu.CompilerParams(
                collective_id=0, has_side_effects=True, vmem_limit_bytes=vmem_bytes
            ),
            name="lora_value_backward",
        )(acts, grad, matrix, down, up, job, live, owner_slot)
        return pl.pallas_call(
            functools.partial(write_out, write_pieces),
            out_shape=tuple(jax.ShapeDtypeStruct(x.shape, x.dtype) for x in results),
            in_specs=[in_hbm] * 3,
            out_specs=(in_hbm,) * 3,
            scratch_shapes=[dma((write_pieces + 2,))],
            compiler_params=pltpu.CompilerParams(vmem_limit_bytes=vmem_bytes),
            name="write_out",
        )(*results)

    placed = (
        P(("rep", "dp"), "tp"),
        P(("rep", "dp"), "tp"),
        P("tp", None),
        P("dp", None, "tp"),
        P("dp", None, "tp"),
        P(("rep", "dp")),
        P(("rep", "dp")),
        P(),
    )
    return jax.shard_map(
        body,
        mesh=mesh,
        in_specs=placed,
        out_specs=(
            P(("rep", "dp"), "tp"),
            P(("rep", "dp"), None, "tp"),
            P(("rep", "dp"), None, "tp"),
        ),
        check_vma=False,
    )
```

```python
import functools

import jax
import jax.numpy as jnp
from jax import lax
from jax.experimental import pallas as pl
from jax.experimental.pallas import tpu as pltpu
from jax.sharding import PartitionSpec as P

adapter_scale = 2.0
cot_chunks = 4
early_chunks = 2
write_pieces = 8
vmem_bytes = 56 * 1024 * 1024
f32 = jnp.float32
bf16 = jnp.bfloat16
MESH = pl.DeviceIdType.MESH
nt = (((1,), (1,)), ((), ()))
nn = (((1,), (0,)), ((), ()))
tn = (((0,), (0,)), ((), ()))


def dot(a, b, dims):
    return lax.dot_general(a, b, dims, preferred_element_type=f32)


def send(src, dst, send_sem, recv_sem, **device):
    return pltpu.make_async_remote_copy(
        src_ref=src,
        dst_ref=dst,
        send_sem=send_sem,
        recv_sem=recv_sem,
        device_id=device,
        device_id_type=MESH,
    )


def kernel(
    reps, owners, parts_tp,
    acts, grad, matrix, down, up, job_h, live_h, owner_slot_h,
    out, grad_down, grad_up,
    job, live, owner_slot, out_v, out_s, act_v, mat_v, cot_v, down_v, up_v,
    back_p, low_p, back_d, back_m, low_m,
    pdown, pup, rdown, rup,
    load_sem, up_s, up_r, dn_s, dn_r, yf_s, yf_r,
    ch_s, ch_r, cl_s, cl_r, cf_s, cf_r,
    bk_s, bk_r, lw_s, lw_r, pd_s, pd_r, pu_s, pu_r,
):
    r = lax.axis_index("rep")
    d = lax.axis_index("dp")
    t = lax.axis_index("tp")
    rows, width = act_v.shape
    rank = down_v.shape[1]
    blocks = job.shape[0]
    block = rows // blocks
    half = blocks // 2
    highs = parts_tp // 2
    hi, lo = t // 2, t % 2
    other = hi * 2 + 1 - lo
    share = rank // reps
    chunk = rows // cot_chunks
    stages = parts_tp.bit_length() - 1

    loads = [
        pltpu.make_async_copy(src, dst, load_sem.at[i])
        for i, (src, dst) in enumerate(
            [
                (job_h, job),
                (live_h, live),
                (owner_slot_h, owner_slot),
                (up.at[0], up_v.at[d]),
                (grad, cot_v.at[t]),
                (down.at[0], down_v.at[d]),
                (acts, act_v),
                (matrix, mat_v),
            ]
        )
    ]
    for load in loads:
        load.start()

    barrier = pltpu.get_barrier_semaphore()
    peers = [{"dp": (d + j) % owners} for j in range(1, owners)]
    peers += [{"tp": ((hi + i) % highs) * 2 + lo} for i in range(1, highs)]
    peers += [{"tp": other}]
    peers += [{"rep": (r + i) % reps} for i in range(1, reps)]
    for peer in peers:
        pl.semaphore_signal(barrier, inc=1, device_id=peer, device_id_type=MESH)
    pl.semaphore_wait(barrier, len(peers))

    up_out = [
        send(up.at[0], up_v.at[d], up_s.at[j], up_r.at[j], dp=(d + j) % owners)
        for j in range(1, owners)
    ]
    for copy in up_out:
        copy.start()

    def cot_rows(c):
        return pl.ds(c * chunk, chunk)

    cot_out = [
        [
            send(
                grad.at[cot_rows(c)], cot_v.at[t, cot_rows(c)], ch_s.at[i, c], ch_r.at[i, c],
                tp=((hi + i) % highs) * 2 + lo,
            )
            for i in range(1, highs)
        ]
        for c in range(cot_chunks)
    ]
    cot_near = send(grad, cot_v.at[t], cl_s, cl_r, tp=other)
    for c in range(early_chunks):
        for copy in cot_out[c]:
            copy.start()
    cot_near.start()

    mine = pl.ds(r * share, share)
    dn_out = [
        send(
            down.at[0, mine], down_v.at[d, mine], dn_s.at[j], dn_r.at[j], dp=(d + j) % owners
        )
        for j in range(1, owners)
    ]
    for copy in dn_out:
        copy.start()

    for load in loads[:5]:
        load.wait()
    slots = [owner_slot[job[b]] for b in range(blocks)]
    lives = [live[b] for b in range(blocks)]

    def stage_copy(buf, s, ss, rs):
        step = 1 << s
        partner = t + step * (1 - 2 * ((t // step) % 2))
        return send(buf.at[2 * s], buf.at[2 * s + 1], ss.at[s], rs.at[s], tp=partner)

    def pack(buf, source, weights, columns):
        for b in range(half):
            pair = []
            for q in (b, b + half):
                weight = weights[slots[q]]
                pair.append(dot(source[pl.ds(q * block, block), :], weight, nt))
            buf[0, pl.ds(b * block, block), :] = jnp.concatenate(pair, 1).astype(bf16)

    def fold(buf, s):
        total = buf[2 * s].astype(f32) + buf[2 * s + 1].astype(f32)
        buf[2 * s + 2] = total.astype(bf16)

    def spread(buf, wide, doubled):
        packed = buf.at[2 * stages]
        for b in range(half):
            pair = packed[pl.ds(b * block, block), :].astype(f32)
            for q, v in ((b, pair[:, :rank]), (b + half, pair[:, rank:])):
                two = jnp.concatenate([v, v], 1)
                rows_q = pl.ds(q * block, block)
                if doubled is not None:
                    doubled[rows_q, :] = two.astype(bf16)
                shape = (block, 2 * rank)
                alive = lax.broadcasted_iota(jnp.int32, shape, 0) < lives[q]
                lane = lax.broadcasted_iota(jnp.int32, shape, 1)
                odd = jnp.where(lane >= rank, 1, 0)
                for k in range(0, owners, 2):
                    keep = jnp.logical_and(alive, odd + k == slots[q])
                    wide[rows_q, pl.ds(k * rank, 2 * rank)] = jnp.where(keep, two, 0.0).astype(bf16)

    for j in range(1, owners):
        src = (d + owners - j) % owners
        send(up.at[0], up_v.at[src], up_s.at[j], up_r.at[j], dp=src).wait_recv()
    pack(back_p, cot_v.at[t], up_v, None)
    stage_copy(back_p, 0, bk_s, bk_r).start()
    for s in range(stages):
        stage_copy(back_p, s, bk_s, bk_r).wait()
        fold(back_p, s)
        if s + 1 < stages:
            stage_copy(back_p, s + 1, bk_s, bk_r).start()
        if s == 0:
            for c in range(early_chunks, cot_chunks):
                for copy in cot_out[c]:
                    copy.start()
    spread(back_p, back_m, back_d)

    group = min(owners, 4)
    loads[6].wait()
    for g in range(0, owners, group):
        lhs = back_m[:, pl.ds(g * rank, group * rank)]
        block_part = adapter_scale * dot(lhs, act_v[...], tn)
        pdown[pl.ds(g, group)] = block_part.astype(bf16).reshape(group, rank, width)
    pd_out = [
        send(
            pdown.at[(d + j) % owners], rdown.at[d], pd_s.at[j], pd_r.at[j], dp=(d + j) % owners
        )
        for j in range(1, owners)
    ]
    for copy in pd_out:
        copy.start()

    loads[5].wait()
    forwards = []
    for j in range(1, owners):
        src = (d + owners - j) % owners
        send(down.at[0, mine], down_v.at[src, mine], dn_s.at[j], dn_r.at[j], dp=src).wait_recv()
        for i in range(1, reps):
            copy = send(
                down_v.at[src, mine], down_v.at[src, mine], yf_s.at[i, j], yf_r.at[i, j],
                rep=(r + i) % reps,
            )
            copy.start()
            forwards.append(copy)

    for c in range(cot_chunks):
        for i in range(1, highs):
            src = ((hi + highs - i) % highs) * 2 + lo
            there = cot_v.at[src, cot_rows(c)]
            send(grad.at[cot_rows(c)], there, ch_s.at[i, c], ch_r.at[i, c], tp=src).wait_recv()
            copy = send(there, there, cf_s.at[i, c], cf_r.at[i, c], tp=other)
            copy.start()
            forwards.append(copy)

    for j in range(1, owners):
        src = (d + owners - j) % owners
        for i in range(1, reps):
            giver = (r + reps - i) % reps
            theirs = down_v.at[src, pl.ds(giver * share, share)]
            send(theirs, theirs, yf_s.at[i, j], yf_r.at[i, j], rep=giver).wait_recv()

    pack(low_p, act_v, down_v, None)
    stage_copy(low_p, 0, lw_s, lw_r).start()

    loads[7].wait()
    cot_near_in = send(grad, cot_v.at[other], cl_s, cl_r, tp=other)
    cot_near_in.wait_recv()
    for c in range(cot_chunks):
        for i in range(1, highs):
            src = ((hi + highs - i) % highs) * 2 + 1 - lo
            there = cot_v.at[src, cot_rows(c)]
            send(there, there, cf_s.at[i, c], cf_r.at[i, c], tp=other).wait_recv()

    def frozen(first, last):
        @pl.loop(first, last)
        def _(b):
            rows_b = pl.ds(pl.multiple_of(b * block, block), block)
            features = jnp.concatenate([cot_v[p, rows_b, :] for p in range(parts_tp)], 1)
            slot = owner_slot[job[b]]
            total = dot(features, mat_v[...], nt)
            total += adapter_scale * dot(back_d[rows_b, :][:, :rank], down_v[slot], nn)
            alive = lax.broadcasted_iota(jnp.int32, (block, width), 0) < live[b]
            out_v[rows_b, :] = jnp.where(alive, total, 0.0).astype(bf16)
            pltpu.make_async_copy(out_v.at[rows_b], out.at[rows_b], out_s.at[b]).start()

    bounds = [blocks * s // (stages + 1) for s in range(stages + 2)]
    for s in range(stages):
        frozen(bounds[s], bounds[s + 1])
        stage_copy(low_p, s, lw_s, lw_r).wait()
        fold(low_p, s)
        if s + 1 < stages:
            stage_copy(low_p, s + 1, lw_s, lw_r).start()
    spread(low_p, low_m, None)

    for g in range(0, owners, group):
        lhs = low_m[:, pl.ds(g * rank, group * rank)]
        block_part = adapter_scale * dot(lhs, cot_v[t], tn)
        pup[pl.ds(g, group)] = block_part.astype(bf16).reshape(group, rank, up_v.shape[2])
    pu_out = [
        send(pup.at[(d + j) % owners], rup.at[d], pu_s.at[j], pu_r.at[j], dp=(d + j) % owners)
        for j in range(1, owners)
    ]
    for copy in pu_out:
        copy.start()
    frozen(bounds[stages], bounds[stages + 1])

    for mine_part, got, ss, rs, result in (
        (pdown, rdown, pd_s, pd_r, grad_down),
        (pup, rup, pu_s, pu_r, grad_up),
    ):
        total = mine_part[d].astype(f32)
        for j in range(1, owners):
            src = (d + owners - j) % owners
            send(mine_part.at[src], got.at[src], ss.at[j], rs.at[j], dp=src).wait_recv()
            total += got[src].astype(f32)
        result[0] = total

    for b in range(blocks):
        rows_b = pl.ds(b * block, block)
        pltpu.make_async_copy(out_v.at[rows_b], out.at[rows_b], out_s.at[b]).wait()
    for copy in up_out + dn_out + pd_out + pu_out + forwards + [cot_near]:
        copy.wait_send()
    for copies in cot_out:
        for copy in copies:
            copy.wait_send()


def write_out(pieces, out_k, down_k, up_k, out, grad_down, grad_up, out_v, down_v, up_v, sem):
    rows = out_k.shape[0] // pieces
    steps = [(out_k, out_v, out)] * pieces + [(down_k, down_v, grad_down), (up_k, up_v, grad_up)]
    reads, writes = [], []
    for i, refs in enumerate(steps):
        if i < pieces:
            refs = [ref.at[pl.ds(i * rows, rows)] for ref in refs]
        reads.append(pltpu.make_async_copy(refs[0], refs[1], sem.at[0, i]))
        writes.append(pltpu.make_async_copy(refs[1], refs[2], sem.at[1, i]))
    for read in reads:
        read.start()
    for read, write in zip(reads, writes):
        read.wait()
        write.start()
    for write in writes:
        write.wait()


def solution(mesh):
    reps, owners, parts_tp = mesh.shape["rep"], mesh.shape["dp"], mesh.shape["tp"]

    def body(acts, grad, matrix, down, up, job, live, owner_slot):
        rows, width = acts.shape
        features = grad.shape[1]
        rank = down.shape[1]
        stages = parts_tp.bit_length() - 1
        highs = parts_tp // 2
        vmem = pltpu.VMEM
        dma = pltpu.SemaphoreType.DMA
        in_hbm = pl.BlockSpec(memory_space=pltpu.HBM)
        in_vmem = pl.BlockSpec(memory_space=pltpu.VMEM)
        packed = vmem((2 * stages + 1, rows // 2, 2 * rank), bf16)
        results = pl.pallas_call(
            functools.partial(kernel, reps, owners, parts_tp),
            out_shape=(
                jax.ShapeDtypeStruct((rows, width), bf16),
                jax.ShapeDtypeStruct((1, rank, width), f32),
                jax.ShapeDtypeStruct((1, rank, features), f32),
            ),
            in_specs=[in_hbm] * 8,
            out_specs=(in_hbm, in_vmem, in_vmem),
            scratch_shapes=[
                pltpu.SMEM(job.shape, jnp.int32),
                pltpu.SMEM(live.shape, jnp.int32),
                pltpu.SMEM(owner_slot.shape, jnp.int32),
                vmem((rows, width), bf16),
                dma(job.shape),
                vmem((rows, width), bf16),
                vmem(matrix.shape, bf16),
                vmem((parts_tp, rows, features), bf16),
                vmem((owners, rank, width), bf16),
                vmem((owners, rank, features), bf16),
                packed,
                packed,
                vmem((rows, 2 * rank), bf16),
                vmem((rows, owners * rank), bf16),
                vmem((rows, owners * rank), bf16),
                vmem((owners, rank, width), bf16),
                vmem((owners, rank, features), bf16),
                vmem((owners, rank, width), bf16),
                vmem((owners, rank, features), bf16),
                dma((8,)),
                dma((owners,)), dma((owners,)),
                dma((owners,)), dma((owners,)),
                dma((reps, owners)), dma((reps, owners)),
                dma((highs, cot_chunks)), dma((highs, cot_chunks)),
                dma, dma,
                dma((highs, cot_chunks)), dma((highs, cot_chunks)),
                dma((stages,)), dma((stages,)),
                dma((stages,)), dma((stages,)),
                dma((owners,)), dma((owners,)),
                dma((owners,)), dma((owners,)),
            ],
            compiler_params=pltpu.CompilerParams(
                collective_id=0, has_side_effects=True, vmem_limit_bytes=vmem_bytes
            ),
            name="lora_value_backward",
        )(acts, grad, matrix, down, up, job, live, owner_slot)
        return pl.pallas_call(
            functools.partial(write_out, write_pieces),
            out_shape=tuple(jax.ShapeDtypeStruct(x.shape, x.dtype) for x in results),
            in_specs=[in_hbm] * 3,
            out_specs=(in_hbm,) * 3,
            scratch_shapes=[vmem(x.shape, x.dtype) for x in results]
            + [dma((2, write_pieces + 2))],
            compiler_params=pltpu.CompilerParams(vmem_limit_bytes=vmem_bytes),
            name="write_out",
        )(*results)

    placed = (
        P(("rep", "dp"), "tp"),
        P(("rep", "dp"), "tp"),
        P("tp", None),
        P("dp", None, "tp"),
        P("dp", None, "tp"),
        P(("rep", "dp")),
        P(("rep", "dp")),
        P(),
    )
    return jax.shard_map(
        body,
        mesh=mesh,
        in_specs=placed,
        out_specs=(
            P(("rep", "dp"), "tp"),
            P(("rep", "dp"), None, "tp"),
            P(("rep", "dp"), None, "tp"),
        ),
        check_vma=False,
    )
```

```python
import functools

import jax
import jax.numpy as jnp
from jax import lax
from jax.experimental import pallas as pl
from jax.experimental.pallas import tpu as pltpu
from jax.sharding import PartitionSpec as P

adapter_scale = 2.0
cot_chunks = 4
early_chunks = 2
write_pieces = 8
vmem_bytes = 56 * 1024 * 1024
f32 = jnp.float32
bf16 = jnp.bfloat16
MESH = pl.DeviceIdType.MESH
nt = (((1,), (1,)), ((), ()))
nn = (((1,), (0,)), ((), ()))
tn = (((0,), (0,)), ((), ()))


def dot(a, b, dims):
    return lax.dot_general(a, b, dims, preferred_element_type=f32)


def send(src, dst, send_sem, recv_sem, **device):
    return pltpu.make_async_remote_copy(
        src_ref=src,
        dst_ref=dst,
        send_sem=send_sem,
        recv_sem=recv_sem,
        device_id=device,
        device_id_type=MESH,
    )


def kernel(
    reps, owners, parts_tp,
    acts, grad, matrix, down, up, job_h, live_h, owner_slot_h,
    out, grad_down, grad_up,
    job, live, owner_slot, out_v, out_s, act_v, mat_v, cot_v, down_v, up_v,
    back_p, back_i, back_t, low_p, low_i, low_t, back_d, back_m, low_m,
    pdown, pup, rdown, rup,
    load_sem, up_s, up_r, dn_s, dn_r, yf_s, yf_r,
    ch_s, ch_r, cl_s, cl_r, cf_s, cf_r,
    bk_s, bk_r, bg_s, bg_r, lw_s, lw_r, lg_s, lg_r, pd_s, pd_r, pu_s, pu_r,
):
    r = lax.axis_index("rep")
    d = lax.axis_index("dp")
    t = lax.axis_index("tp")
    rows, width = act_v.shape
    rank = down_v.shape[1]
    blocks = job.shape[0]
    block = rows // blocks
    half = blocks // 2
    highs = parts_tp // 2
    hi, lo = t // 2, t % 2
    other = hi * 2 + 1 - lo
    share = rank // reps
    chunk = rows // cot_chunks
    seg = half * block // parts_tp

    loads = [
        pltpu.make_async_copy(src, dst, load_sem.at[i])
        for i, (src, dst) in enumerate(
            [
                (job_h, job),
                (live_h, live),
                (owner_slot_h, owner_slot),
                (up.at[0], up_v.at[d]),
                (grad, cot_v.at[t]),
                (down.at[0], down_v.at[d]),
                (acts, act_v),
                (matrix, mat_v),
            ]
        )
    ]
    for load in loads:
        load.start()

    barrier = pltpu.get_barrier_semaphore()
    peers = [{"dp": (d + j) % owners} for j in range(1, owners)]
    peers += [{"tp": (t + i) % parts_tp} for i in range(1, parts_tp)]
    peers += [{"rep": (r + i) % reps} for i in range(1, reps)]
    for peer in peers:
        pl.semaphore_signal(barrier, inc=1, device_id=peer, device_id_type=MESH)
    pl.semaphore_wait(barrier, len(peers))

    up_out = [
        send(up.at[0], up_v.at[d], up_s.at[j], up_r.at[j], dp=(d + j) % owners)
        for j in range(1, owners)
    ]
    for copy in up_out:
        copy.start()

    def cot_rows(c):
        return pl.ds(c * chunk, chunk)

    cot_out = [
        [
            send(
                grad.at[cot_rows(c)], cot_v.at[t, cot_rows(c)], ch_s.at[i, c], ch_r.at[i, c],
                tp=((hi + i) % highs) * 2 + lo,
            )
            for i in range(1, highs)
        ]
        for c in range(cot_chunks)
    ]
    cot_near = send(grad, cot_v.at[t], cl_s, cl_r, tp=other)
    for c in range(early_chunks):
        for copy in cot_out[c]:
            copy.start()
    cot_near.start()

    mine = pl.ds(r * share, share)
    dn_out = [
        send(
            down.at[0, mine], down_v.at[d, mine], dn_s.at[j], dn_r.at[j], dp=(d + j) % owners
        )
        for j in range(1, owners)
    ]
    for copy in dn_out:
        copy.start()

    for load in loads[:5]:
        load.wait()
    slots = [owner_slot[job[b]] for b in range(blocks)]
    lives = [live[b] for b in range(blocks)]

    def segment(p):
        return pl.ds(pl.multiple_of(p * seg, seg), seg)

    def scatter(part, got, ss, rs):
        return [
            send(
                part.at[segment((t + i) % parts_tp)], got.at[t], ss.at[i], rs.at[i],
                tp=(t + i) % parts_tp,
            )
            for i in range(1, parts_tp)
        ]

    def gather(whole, ss, rs):
        return [
            send(
                whole.at[segment(t)], whole.at[segment(t)], ss.at[i], rs.at[i],
                tp=(t + i) % parts_tp,
            )
            for i in range(1, parts_tp)
        ]

    def reduce(part, got, whole, ss, rs):
        total = part[segment(t), :].astype(f32)
        for i in range(1, parts_tp):
            src = (t + parts_tp - i) % parts_tp
            send(part.at[segment(src)], got.at[src], ss.at[i], rs.at[i], tp=src).wait_recv()
            total += got[src].astype(f32)
        whole[segment(t), :] = total.astype(bf16)

    def gathered(whole, ss, rs):
        for i in range(1, parts_tp):
            src = (t + parts_tp - i) % parts_tp
            there = whole.at[segment(src)]
            send(there, there, ss.at[i], rs.at[i], tp=src).wait_recv()

    def pack(buf, source, weights):
        for b in range(half):
            pair = []
            for q in (b, b + half):
                weight = weights[slots[q]]
                pair.append(dot(source[pl.ds(q * block, block), :], weight, nt))
            buf[pl.ds(b * block, block), :] = jnp.concatenate(pair, 1).astype(bf16)

    def spread(packed, wide, doubled):
        for b in range(half):
            pair = packed[pl.ds(b * block, block), :].astype(f32)
            for q, v in ((b, pair[:, :rank]), (b + half, pair[:, rank:])):
                two = jnp.concatenate([v, v], 1)
                rows_q = pl.ds(q * block, block)
                if doubled is not None:
                    doubled[rows_q, :] = two.astype(bf16)
                shape = (block, 2 * rank)
                alive = lax.broadcasted_iota(jnp.int32, shape, 0) < lives[q]
                lane = lax.broadcasted_iota(jnp.int32, shape, 1)
                odd = jnp.where(lane >= rank, 1, 0)
                for k in range(0, owners, 2):
                    keep = jnp.logical_and(alive, odd + k == slots[q])
                    wide[rows_q, pl.ds(k * rank, 2 * rank)] = jnp.where(keep, two, 0.0).astype(bf16)

    for j in range(1, owners):
        src = (d + owners - j) % owners
        send(up.at[0], up_v.at[src], up_s.at[j], up_r.at[j], dp=src).wait_recv()
    pack(back_p, cot_v.at[t], up_v)
    sums = scatter(back_p, back_i, bk_s, bk_r)
    for copy in sums:
        copy.start()
    reduce(back_p, back_i, back_t, bk_s, bk_r)
    back_out = gather(back_t, bg_s, bg_r)
    for copy in back_out:
        copy.start()
    sums += back_out
    for c in range(early_chunks, cot_chunks):
        for copy in cot_out[c]:
            copy.start()
    gathered(back_t, bg_s, bg_r)
    spread(back_t, back_m, back_d)

    group = min(owners, 4)
    loads[6].wait()
    for g in range(0, owners, group):
        lhs = back_m[:, pl.ds(g * rank, group * rank)]
        block_part = adapter_scale * dot(lhs, act_v[...], tn)
        pdown[pl.ds(g, group)] = block_part.astype(bf16).reshape(group, rank, width)
    pd_out = [
        send(
            pdown.at[(d + j) % owners], rdown.at[d], pd_s.at[j], pd_r.at[j], dp=(d + j) % owners
        )
        for j in range(1, owners)
    ]
    for copy in pd_out:
        copy.start()

    loads[5].wait()
    forwards = []
    for j in range(1, owners):
        src = (d + owners - j) % owners
        send(down.at[0, mine], down_v.at[src, mine], dn_s.at[j], dn_r.at[j], dp=src).wait_recv()
        for i in range(1, reps):
            copy = send(
                down_v.at[src, mine], down_v.at[src, mine], yf_s.at[i, j], yf_r.at[i, j],
                rep=(r + i) % reps,
            )
            copy.start()
            forwards.append(copy)

    def pass_on(c):
        for i in range(1, highs):
            src = ((hi + highs - i) % highs) * 2 + lo
            there = cot_v.at[src, cot_rows(c)]
            send(grad.at[cot_rows(c)], there, ch_s.at[i, c], ch_r.at[i, c], tp=src).wait_recv()
            copy = send(there, there, cf_s.at[i, c], cf_r.at[i, c], tp=other)
            copy.start()
            forwards.append(copy)

    for c in range(early_chunks):
        pass_on(c)

    for j in range(1, owners):
        src = (d + owners - j) % owners
        for i in range(1, reps):
            giver = (r + reps - i) % reps
            theirs = down_v.at[src, pl.ds(giver * share, share)]
            send(theirs, theirs, yf_s.at[i, j], yf_r.at[i, j], rep=giver).wait_recv()

    pack(low_p, act_v, down_v)
    low_sums = scatter(low_p, low_i, lw_s, lw_r)
    for copy in low_sums:
        copy.start()
    sums += low_sums
    for c in range(early_chunks, cot_chunks):
        pass_on(c)

    loads[7].wait()
    send(grad, cot_v.at[other], cl_s, cl_r, tp=other).wait_recv()

    def frozen(c):
        for i in range(1, highs):
            src = ((hi + highs - i) % highs) * 2 + 1 - lo
            there = cot_v.at[src, cot_rows(c)]
            send(there, there, cf_s.at[i, c], cf_r.at[i, c], tp=other).wait_recv()

        @pl.loop(c * blocks // cot_chunks, (c + 1) * blocks // cot_chunks)
        def _(b):
            rows_b = pl.ds(pl.multiple_of(b * block, block), block)
            features = jnp.concatenate([cot_v[p, rows_b, :] for p in range(parts_tp)], 1)
            slot = owner_slot[job[b]]
            total = dot(features, mat_v[...], nt)
            total += adapter_scale * dot(back_d[rows_b, :][:, :rank], down_v[slot], nn)
            alive = lax.broadcasted_iota(jnp.int32, (block, width), 0) < live[b]
            out_v[rows_b, :] = jnp.where(alive, total, 0.0).astype(bf16)
            pltpu.make_async_copy(out_v.at[rows_b], out.at[rows_b], out_s.at[b]).start()

    frozen(0)
    reduce(low_p, low_i, low_t, lw_s, lw_r)
    low_out = gather(low_t, lg_s, lg_r)
    for copy in low_out:
        copy.start()
    sums += low_out
    frozen(1)
    gathered(low_t, lg_s, lg_r)
    spread(low_t, low_m, None)

    for g in range(0, owners, group):
        lhs = low_m[:, pl.ds(g * rank, group * rank)]
        block_part = adapter_scale * dot(lhs, cot_v[t], tn)
        pup[pl.ds(g, group)] = block_part.astype(bf16).reshape(group, rank, up_v.shape[2])
    pu_out = [
        send(pup.at[(d + j) % owners], rup.at[d], pu_s.at[j], pu_r.at[j], dp=(d + j) % owners)
        for j in range(1, owners)
    ]
    for copy in pu_out:
        copy.start()
    for c in range(2, cot_chunks):
        frozen(c)

    for mine_part, got, ss, rs, result in (
        (pdown, rdown, pd_s, pd_r, grad_down),
        (pup, rup, pu_s, pu_r, grad_up),
    ):
        total = mine_part[d].astype(f32)
        for j in range(1, owners):
            src = (d + owners - j) % owners
            send(mine_part.at[src], got.at[src], ss.at[j], rs.at[j], dp=src).wait_recv()
            total += got[src].astype(f32)
        result[0] = total

    for b in range(blocks):
        rows_b = pl.ds(b * block, block)
        pltpu.make_async_copy(out_v.at[rows_b], out.at[rows_b], out_s.at[b]).wait()
    for copy in up_out + dn_out + pd_out + pu_out + forwards + sums + [cot_near]:
        copy.wait_send()
    for copies in cot_out:
        for copy in copies:
            copy.wait_send()


def write_out(pieces, out_k, down_k, up_k, out, grad_down, grad_up, out_v, down_v, up_v, sem):
    rows = out_k.shape[0] // pieces
    steps = [(out_k, out_v, out)] * pieces + [(down_k, down_v, grad_down), (up_k, up_v, grad_up)]
    reads, writes = [], []
    for i, refs in enumerate(steps):
        if i < pieces:
            refs = [ref.at[pl.ds(i * rows, rows)] for ref in refs]
        reads.append(pltpu.make_async_copy(refs[0], refs[1], sem.at[0, i]))
        writes.append(pltpu.make_async_copy(refs[1], refs[2], sem.at[1, i]))
    for read in reads:
        read.start()
    for read, write in zip(reads, writes):
        read.wait()
        write.start()
    for write in writes:
        write.wait()


def solution(mesh):
    reps, owners, parts_tp = mesh.shape["rep"], mesh.shape["dp"], mesh.shape["tp"]

    def body(acts, grad, matrix, down, up, job, live, owner_slot):
        rows, width = acts.shape
        features = grad.shape[1]
        rank = down.shape[1]
        highs = parts_tp // 2
        vmem = pltpu.VMEM
        dma = pltpu.SemaphoreType.DMA
        in_hbm = pl.BlockSpec(memory_space=pltpu.HBM)
        in_vmem = pl.BlockSpec(memory_space=pltpu.VMEM)
        packed = vmem((rows // 2, 2 * rank), bf16)
        segments = vmem((parts_tp, rows // 2 // parts_tp, 2 * rank), bf16)
        results = pl.pallas_call(
            functools.partial(kernel, reps, owners, parts_tp),
            out_shape=(
                jax.ShapeDtypeStruct((rows, width), bf16),
                jax.ShapeDtypeStruct((1, rank, width), f32),
                jax.ShapeDtypeStruct((1, rank, features), f32),
            ),
            in_specs=[in_hbm] * 8,
            out_specs=(in_hbm, in_vmem, in_vmem),
            scratch_shapes=[
                pltpu.SMEM(job.shape, jnp.int32),
                pltpu.SMEM(live.shape, jnp.int32),
                pltpu.SMEM(owner_slot.shape, jnp.int32),
                vmem((rows, width), bf16),
                dma(job.shape),
                vmem((rows, width), bf16),
                vmem(matrix.shape, bf16),
                vmem((parts_tp, rows, features), bf16),
                vmem((owners, rank, width), bf16),
                vmem((owners, rank, features), bf16),
                packed, segments, packed,
                packed, segments, packed,
                vmem((rows, 2 * rank), bf16),
                vmem((rows, owners * rank), bf16),
                vmem((rows, owners * rank), bf16),
                vmem((owners, rank, width), bf16),
                vmem((owners, rank, features), bf16),
                vmem((owners, rank, width), bf16),
                vmem((owners, rank, features), bf16),
                dma((8,)),
                dma((owners,)), dma((owners,)),
                dma((owners,)), dma((owners,)),
                dma((reps, owners)), dma((reps, owners)),
                dma((highs, cot_chunks)), dma((highs, cot_chunks)),
                dma, dma,
                dma((highs, cot_chunks)), dma((highs, cot_chunks)),
                dma((parts_tp,)), dma((parts_tp,)),
                dma((parts_tp,)), dma((parts_tp,)),
                dma((parts_tp,)), dma((parts_tp,)),
                dma((parts_tp,)), dma((parts_tp,)),
                dma((owners,)), dma((owners,)),
                dma((owners,)), dma((owners,)),
            ],
            compiler_params=pltpu.CompilerParams(
                collective_id=0, has_side_effects=True, vmem_limit_bytes=vmem_bytes
            ),
            name="lora_value_backward",
        )(acts, grad, matrix, down, up, job, live, owner_slot)
        return pl.pallas_call(
            functools.partial(write_out, write_pieces),
            out_shape=tuple(jax.ShapeDtypeStruct(x.shape, x.dtype) for x in results),
            in_specs=[in_hbm] * 3,
            out_specs=(in_hbm,) * 3,
            scratch_shapes=[vmem(x.shape, x.dtype) for x in results]
            + [dma((2, write_pieces + 2))],
            compiler_params=pltpu.CompilerParams(vmem_limit_bytes=vmem_bytes),
            name="write_out",
        )(*results)

    placed = (
        P(("rep", "dp"), "tp"),
        P(("rep", "dp"), "tp"),
        P("tp", None),
        P("dp", None, "tp"),
        P("dp", None, "tp"),
        P(("rep", "dp")),
        P(("rep", "dp")),
        P(),
    )
    return jax.shard_map(
        body,
        mesh=mesh,
        in_specs=placed,
        out_specs=(
            P(("rep", "dp"), "tp"),
            P(("rep", "dp"), None, "tp"),
            P(("rep", "dp"), None, "tp"),
        ),
        check_vma=False,
    )
```

```python
import functools

import jax
import jax.numpy as jnp
from jax import lax
from jax.experimental import pallas as pl
from jax.experimental.pallas import tpu as pltpu
from jax.sharding import PartitionSpec as P

adapter_scale = 2.0
cot_chunks = 4
write_pieces = 8
vmem_bytes = 56 * 1024 * 1024
f32 = jnp.float32
bf16 = jnp.bfloat16
MESH = pl.DeviceIdType.MESH
nt = (((1,), (1,)), ((), ()))
nn = (((1,), (0,)), ((), ()))
tn = (((0,), (0,)), ((), ()))


def dot(a, b, dims):
    return lax.dot_general(a, b, dims, preferred_element_type=f32)


def send(src, dst, send_sem, recv_sem, **device):
    return pltpu.make_async_remote_copy(
        src_ref=src,
        dst_ref=dst,
        send_sem=send_sem,
        recv_sem=recv_sem,
        device_id=device,
        device_id_type=MESH,
    )


def kernel(
    reps, owners, parts_tp,
    acts, grad, matrix, down, up, job_h, live_h, owner_slot_h,
    out, grad_down, grad_up,
    job, live, owner_slot, out_v, out_s, act_v, mat_v, cot_v, down_v, up_v,
    back_p, back_i, back_t, low_p, low_i, low_t, back_d, back_m, low_m,
    pdown, pup, rdown, rup,
    load_sem, up_s, up_r, dn_s, dn_r, yf_s, yf_r,
    ch_s, ch_r, cl_s, cl_r, cf_s, cf_r,
    bk_s, bk_r, bg_s, bg_r, lw_s, lw_r, lg_s, lg_r, pd_s, pd_r, pu_s, pu_r,
):
    r = lax.axis_index("rep")
    d = lax.axis_index("dp")
    t = lax.axis_index("tp")
    rows, width = act_v.shape
    rank = down_v.shape[1]
    blocks = job.shape[0]
    block = rows // blocks
    half = blocks // 2
    highs = parts_tp // 2
    hi, lo = t // 2, t % 2
    other = hi * 2 + 1 - lo
    share = rank // reps
    chunk = rows // cot_chunks
    seg = half * block // parts_tp

    loads = [
        pltpu.make_async_copy(src, dst, load_sem.at[i])
        for i, (src, dst) in enumerate(
            [
                (job_h, job),
                (live_h, live),
                (owner_slot_h, owner_slot),
                (up.at[0], up_v.at[d]),
                (grad, cot_v.at[t]),
                (down.at[0], down_v.at[d]),
                (acts, act_v),
                (matrix, mat_v),
            ]
        )
    ]
    for load in loads:
        load.start()

    barrier = pltpu.get_barrier_semaphore()
    peers = [{"dp": (d + j) % owners} for j in range(1, owners)]
    peers += [{"tp": (t + i) % parts_tp} for i in range(1, parts_tp)]
    peers += [{"rep": (r + i) % reps} for i in range(1, reps)]
    for peer in peers:
        pl.semaphore_signal(barrier, inc=1, device_id=peer, device_id_type=MESH)
    pl.semaphore_wait(barrier, len(peers))

    up_out = [
        send(up.at[0], up_v.at[d], up_s.at[j], up_r.at[j], dp=(d + j) % owners)
        for j in range(1, owners)
    ]
    for copy in up_out:
        copy.start()

    def cot_rows(c):
        return pl.ds(c * chunk, chunk)

    cot_out = [
        [
            send(
                grad.at[cot_rows(c)], cot_v.at[t, cot_rows(c)], ch_s.at[i, c], ch_r.at[i, c],
                tp=((hi + i) % highs) * 2 + lo,
            )
            for i in range(1, highs)
        ]
        for c in range(cot_chunks)
    ]
    cot_near = send(grad, cot_v.at[t], cl_s, cl_r, tp=other)
    cot_near.start()

    mine = pl.ds(r * share, share)
    dn_out = [
        send(
            down.at[0, mine], down_v.at[d, mine], dn_s.at[j], dn_r.at[j], dp=(d + j) % owners
        )
        for j in range(1, owners)
    ]
    for copy in dn_out:
        copy.start()

    for load in loads[:5]:
        load.wait()
    slots = [owner_slot[job[b]] for b in range(blocks)]
    lives = [live[b] for b in range(blocks)]

    def segment(p):
        return pl.ds(pl.multiple_of(p * seg, seg), seg)

    def scatter(part, got, ss, rs):
        return [
            send(
                part.at[segment((t + i) % parts_tp)], got.at[t], ss.at[i], rs.at[i],
                tp=(t + i) % parts_tp,
            )
            for i in range(1, parts_tp)
        ]

    def gather(whole, ss, rs):
        return [
            send(
                whole.at[segment(t)], whole.at[segment(t)], ss.at[i], rs.at[i],
                tp=(t + i) % parts_tp,
            )
            for i in range(1, parts_tp)
        ]

    def reduce(part, got, whole, ss, rs):
        total = part[segment(t), :].astype(f32)
        for i in range(1, parts_tp):
            src = (t + parts_tp - i) % parts_tp
            send(part.at[segment(src)], got.at[src], ss.at[i], rs.at[i], tp=src).wait_recv()
            total += got[src].astype(f32)
        whole[segment(t), :] = total.astype(bf16)

    def gathered(whole, ss, rs):
        for i in range(1, parts_tp):
            src = (t + parts_tp - i) % parts_tp
            there = whole.at[segment(src)]
            send(there, there, ss.at[i], rs.at[i], tp=src).wait_recv()

    def pack(buf, source, weights):
        for b in range(half):
            pair = []
            for q in (b, b + half):
                weight = weights[slots[q]]
                pair.append(dot(source[pl.ds(q * block, block), :], weight, nt))
            buf[pl.ds(b * block, block), :] = jnp.concatenate(pair, 1).astype(bf16)

    def spread(packed, wide, doubled):
        for b in range(half):
            pair = packed[pl.ds(b * block, block), :].astype(f32)
            for q, v in ((b, pair[:, :rank]), (b + half, pair[:, rank:])):
                two = jnp.concatenate([v, v], 1)
                rows_q = pl.ds(q * block, block)
                if doubled is not None:
                    doubled[rows_q, :] = two.astype(bf16)
                shape = (block, 2 * rank)
                alive = lax.broadcasted_iota(jnp.int32, shape, 0) < lives[q]
                lane = lax.broadcasted_iota(jnp.int32, shape, 1)
                odd = jnp.where(lane >= rank, 1, 0)
                for k in range(0, owners, 2):
                    keep = jnp.logical_and(alive, odd + k == slots[q])
                    wide[rows_q, pl.ds(k * rank, 2 * rank)] = jnp.where(keep, two, 0.0).astype(bf16)

    for j in range(1, owners):
        src = (d + owners - j) % owners
        send(up.at[0], up_v.at[src], up_s.at[j], up_r.at[j], dp=src).wait_recv()
    pack(back_p, cot_v.at[t], up_v)
    sums = scatter(back_p, back_i, bk_s, bk_r)
    for copy in sums:
        copy.start()
    reduce(back_p, back_i, back_t, bk_s, bk_r)
    back_out = gather(back_t, bg_s, bg_r)
    for copy in back_out:
        copy.start()
    sums += back_out
    for c in range(cot_chunks):
        for copy in cot_out[c]:
            copy.start()
    gathered(back_t, bg_s, bg_r)
    spread(back_t, back_m, back_d)

    group = min(owners, 4)
    loads[6].wait()
    for g in range(0, owners, group):
        lhs = back_m[:, pl.ds(g * rank, group * rank)]
        block_part = adapter_scale * dot(lhs, act_v[...], tn)
        pdown[pl.ds(g, group)] = block_part.astype(bf16).reshape(group, rank, width)
    pd_out = [
        send(
            pdown.at[(d + j) % owners], rdown.at[d], pd_s.at[j], pd_r.at[j], dp=(d + j) % owners
        )
        for j in range(1, owners)
    ]
    for copy in pd_out:
        copy.start()

    loads[5].wait()
    forwards = []
    for j in range(1, owners):
        src = (d + owners - j) % owners
        send(down.at[0, mine], down_v.at[src, mine], dn_s.at[j], dn_r.at[j], dp=src).wait_recv()
        for i in range(1, reps):
            copy = send(
                down_v.at[src, mine], down_v.at[src, mine], yf_s.at[i, j], yf_r.at[i, j],
                rep=(r + i) % reps,
            )
            copy.start()
            forwards.append(copy)

    def pass_on(c):
        for i in range(1, highs):
            src = ((hi + highs - i) % highs) * 2 + lo
            there = cot_v.at[src, cot_rows(c)]
            send(grad.at[cot_rows(c)], there, ch_s.at[i, c], ch_r.at[i, c], tp=src).wait_recv()
            copy = send(there, there, cf_s.at[i, c], cf_r.at[i, c], tp=other)
            copy.start()
            forwards.append(copy)

    for j in range(1, owners):
        src = (d + owners - j) % owners
        for i in range(1, reps):
            giver = (r + reps - i) % reps
            theirs = down_v.at[src, pl.ds(giver * share, share)]
            send(theirs, theirs, yf_s.at[i, j], yf_r.at[i, j], rep=giver).wait_recv()

    pack(low_p, act_v, down_v)
    low_sums = scatter(low_p, low_i, lw_s, lw_r)
    for copy in low_sums:
        copy.start()
    sums += low_sums
    pass_on(0)

    loads[7].wait()
    send(grad, cot_v.at[other], cl_s, cl_r, tp=other).wait_recv()

    def frozen(c):
        for i in range(1, highs):
            src = ((hi + highs - i) % highs) * 2 + 1 - lo
            there = cot_v.at[src, cot_rows(c)]
            send(there, there, cf_s.at[i, c], cf_r.at[i, c], tp=other).wait_recv()

        @pl.loop(c * blocks // cot_chunks, (c + 1) * blocks // cot_chunks)
        def _(b):
            rows_b = pl.ds(pl.multiple_of(b * block, block), block)
            features = jnp.concatenate([cot_v[p, rows_b, :] for p in range(parts_tp)], 1)
            slot = owner_slot[job[b]]
            total = dot(features, mat_v[...], nt)
            total += adapter_scale * dot(back_d[rows_b, :][:, :rank], down_v[slot], nn)
            alive = lax.broadcasted_iota(jnp.int32, (block, width), 0) < live[b]
            out_v[rows_b, :] = jnp.where(alive, total, 0.0).astype(bf16)
            pltpu.make_async_copy(out_v.at[rows_b], out.at[rows_b], out_s.at[b]).start()

    reduce(low_p, low_i, low_t, lw_s, lw_r)
    low_out = gather(low_t, lg_s, lg_r)
    for copy in low_out:
        copy.start()
    sums += low_out
    for c in range(1, cot_chunks - 1):
        pass_on(c)
    gathered(low_t, lg_s, lg_r)
    spread(low_t, low_m, None)

    for g in range(0, owners, group):
        lhs = low_m[:, pl.ds(g * rank, group * rank)]
        block_part = adapter_scale * dot(lhs, cot_v[t], tn)
        pup[pl.ds(g, group)] = block_part.astype(bf16).reshape(group, rank, up_v.shape[2])
    pu_out = [
        send(pup.at[(d + j) % owners], rup.at[d], pu_s.at[j], pu_r.at[j], dp=(d + j) % owners)
        for j in range(1, owners)
    ]
    for copy in pu_out:
        copy.start()
    pass_on(cot_chunks - 1)
    for c in range(cot_chunks):
        frozen(c)

    for mine_part, got, ss, rs, result in (
        (pdown, rdown, pd_s, pd_r, grad_down),
        (pup, rup, pu_s, pu_r, grad_up),
    ):
        total = mine_part[d].astype(f32)
        for j in range(1, owners):
            src = (d + owners - j) % owners
            send(mine_part.at[src], got.at[src], ss.at[j], rs.at[j], dp=src).wait_recv()
            total += got[src].astype(f32)
        result[0] = total

    for b in range(blocks):
        rows_b = pl.ds(b * block, block)
        pltpu.make_async_copy(out_v.at[rows_b], out.at[rows_b], out_s.at[b]).wait()
    for copy in up_out + dn_out + pd_out + pu_out + forwards + sums + [cot_near]:
        copy.wait_send()
    for copies in cot_out:
        for copy in copies:
            copy.wait_send()


def write_out(pieces, out_k, down_k, up_k, out, grad_down, grad_up, out_v, down_v, up_v, sem):
    rows = out_k.shape[0] // pieces
    steps = [(out_k, out_v, out)] * pieces + [(down_k, down_v, grad_down), (up_k, up_v, grad_up)]
    reads, writes = [], []
    for i, refs in enumerate(steps):
        if i < pieces:
            refs = [ref.at[pl.ds(i * rows, rows)] for ref in refs]
        reads.append(pltpu.make_async_copy(refs[0], refs[1], sem.at[0, i]))
        writes.append(pltpu.make_async_copy(refs[1], refs[2], sem.at[1, i]))
    for read in reads:
        read.start()
    for read, write in zip(reads, writes):
        read.wait()
        write.start()
    for write in writes:
        write.wait()


def solution(mesh):
    reps, owners, parts_tp = mesh.shape["rep"], mesh.shape["dp"], mesh.shape["tp"]

    def body(acts, grad, matrix, down, up, job, live, owner_slot):
        rows, width = acts.shape
        features = grad.shape[1]
        rank = down.shape[1]
        highs = parts_tp // 2
        vmem = pltpu.VMEM
        dma = pltpu.SemaphoreType.DMA
        in_hbm = pl.BlockSpec(memory_space=pltpu.HBM)
        in_vmem = pl.BlockSpec(memory_space=pltpu.VMEM)
        packed = vmem((rows // 2, 2 * rank), bf16)
        segments = vmem((parts_tp, rows // 2 // parts_tp, 2 * rank), bf16)
        results = pl.pallas_call(
            functools.partial(kernel, reps, owners, parts_tp),
            out_shape=(
                jax.ShapeDtypeStruct((rows, width), bf16),
                jax.ShapeDtypeStruct((1, rank, width), f32),
                jax.ShapeDtypeStruct((1, rank, features), f32),
            ),
            in_specs=[in_hbm] * 8,
            out_specs=(in_hbm, in_vmem, in_vmem),
            scratch_shapes=[
                pltpu.SMEM(job.shape, jnp.int32),
                pltpu.SMEM(live.shape, jnp.int32),
                pltpu.SMEM(owner_slot.shape, jnp.int32),
                vmem((rows, width), bf16),
                dma(job.shape),
                vmem((rows, width), bf16),
                vmem(matrix.shape, bf16),
                vmem((parts_tp, rows, features), bf16),
                vmem((owners, rank, width), bf16),
                vmem((owners, rank, features), bf16),
                packed, segments, packed,
                packed, segments, packed,
                vmem((rows, 2 * rank), bf16),
                vmem((rows, owners * rank), bf16),
                vmem((rows, owners * rank), bf16),
                vmem((owners, rank, width), bf16),
                vmem((owners, rank, features), bf16),
                vmem((owners, rank, width), bf16),
                vmem((owners, rank, features), bf16),
                dma((8,)),
                dma((owners,)), dma((owners,)),
                dma((owners,)), dma((owners,)),
                dma((reps, owners)), dma((reps, owners)),
                dma((highs, cot_chunks)), dma((highs, cot_chunks)),
                dma, dma,
                dma((highs, cot_chunks)), dma((highs, cot_chunks)),
                dma((parts_tp,)), dma((parts_tp,)),
                dma((parts_tp,)), dma((parts_tp,)),
                dma((parts_tp,)), dma((parts_tp,)),
                dma((parts_tp,)), dma((parts_tp,)),
                dma((owners,)), dma((owners,)),
                dma((owners,)), dma((owners,)),
            ],
            compiler_params=pltpu.CompilerParams(
                collective_id=0, has_side_effects=True, vmem_limit_bytes=vmem_bytes
            ),
            name="lora_value_backward",
        )(acts, grad, matrix, down, up, job, live, owner_slot)
        return pl.pallas_call(
            functools.partial(write_out, write_pieces),
            out_shape=tuple(jax.ShapeDtypeStruct(x.shape, x.dtype) for x in results),
            in_specs=[in_hbm] * 3,
            out_specs=(in_hbm,) * 3,
            scratch_shapes=[vmem(x.shape, x.dtype) for x in results]
            + [dma((2, write_pieces + 2))],
            compiler_params=pltpu.CompilerParams(vmem_limit_bytes=vmem_bytes),
            name="write_out",
        )(*results)

    placed = (
        P(("rep", "dp"), "tp"),
        P(("rep", "dp"), "tp"),
        P("tp", None),
        P("dp", None, "tp"),
        P("dp", None, "tp"),
        P(("rep", "dp")),
        P(("rep", "dp")),
        P(),
    )
    return jax.shard_map(
        body,
        mesh=mesh,
        in_specs=placed,
        out_specs=(
            P(("rep", "dp"), "tp"),
            P(("rep", "dp"), None, "tp"),
            P(("rep", "dp"), None, "tp"),
        ),
        check_vma=False,
    )
```
